512 devices in a mesh: pool: 4 (over x), seq: 16 (over z, core), tp: 8 (over y).
Axes of the slice: x: 4, y: 8, z: 8, core: 2. Of those that a mesh axis runs over, the one named last changes fastest.
Arguments:
- queries: bfloat16 [64, 256, 8192], P(('pool', 'seq'), 'tp')
- stretch_kv: bfloat16 [64, 256, 8, 256], P(('pool', 'seq'), 'tp')
- pool_kv: bfloat16 [1024, 128, 8, 256], P(('pool', 'seq'), None, 'tp'), may hold values from -6 to 6
- prefix_blocks: int32 [64], replicated, may hold values from 24 to 48
- block_owner: int32 [64, 48], replicated, may hold values from 0 to 63, as said below
- block_slot: int32 [64, 48], replicated, may hold values from 0 to 15
Outputs:
- attended: bfloat16 [64, 256, 8192], P(('pool', 'seq'), 'tp')
The draws below stay inside these ranges and needn't reach their ends.
Inputs may be any that keep to these rules, and one draw needn't show every extreme that they name: `block_owner`: among the first prefix_blocks[r] entries of row r no owner is named more than 1 times, and some request names one owner exactly 1 times.
All inputs are finite; a program needn't handle non-finite values.
Results may differ from the reference program's by a relative error of at most 0.005.
Values may be sent and summed in bfloat16 or wider, within the bound.
No kernel may reach another device: no remote copies, remote signals or barrier semaphores. Data moves between devices by JAX's collectives and lax.ppermute only.
A program may use at most 64 MiB of HBM per device.

```python
import math
import jax
import jax.numpy as jnp
from jax import lax

QH = 64
KVH = 8
HD = 128
BLK = 128
MINB = 24
MAXB = 48
STRETCH = 256
SLOTS = 16
OWNERS = 64
REQS = 64


def shared_keys(key):
    return jax.random.normal(key, (REQS, STRETCH, KVH, HD), jnp.float32)


def draw_stretch_kv(key, part):
    shared = shared_keys(key)
    key = jax.random.fold_in(key, 21)
    key_values = jax.random.fold_in(key, 0)
    values = jax.random.normal(key_values, (REQS, STRETCH, KVH, HD), jnp.float32)
    key_part = shared
    return jnp.concatenate([key_part, values], axis=-1).astype(jnp.bfloat16)


def draw_queries(key, part):
    key = jax.random.fold_in(key, 22)
    normal_part = 3.0 * jax.random.normal(key, (REQS, STRETCH, QH * HD), jnp.float32)
    return normal_part.astype(jnp.bfloat16)


def draw_prefix_blocks(key, part):
    key = jax.random.fold_in(key, 11)
    key_first, key_long = jax.random.split(key, 2)
    lengths = jax.random.randint(key_first, (REQS,), MINB, MAXB + 1)
    longest = jax.random.randint(key_long, (), 0, REQS)
    return jnp.where(jnp.arange(REQS) == longest, MAXB, lengths).astype(jnp.int32)


def draw_block_owner(key, part):
    key = jax.random.fold_in(key, 12)
    row_keys = jax.random.split(key, REQS)
    shuffled = jax.vmap(lambda row_key: jax.random.permutation(row_key, OWNERS))(row_keys)
    column = jnp.arange(MAXB) % OWNERS
    return shuffled[:, column].astype(jnp.int32)


def set_ends(drawn, key, low, high):
    extent = drawn.shape
    place = [jax.random.randint(jax.random.fold_in(key, axis), (), 0, extent[axis]) for axis in range(len(extent))]
    drawn = drawn.at[tuple(place)].set(low)
    longest = extent.index(max(extent))
    place[longest] = (place[longest] + 1) % extent[longest]
    return drawn.at[tuple(place)].set(high)


def block_levels(stream_key, extent, pieces, low, top_value):
    gain = 1.0
    for axis_at, shards_of in pieces:
        steps = jax.random.uniform(jax.random.fold_in(jax.random.fold_in(stream_key, 6), axis_at), (shards_of,), jnp.float32, low / len(pieces), top_value / len(pieces))
        gain = gain * jnp.repeat(jnp.exp(steps), extent[axis_at] // shards_of).reshape((-1,) + (1,) * (len(extent) - 1 - axis_at))
    return gain


def centred(key, shape, deviation, reach, cuts=(), held_as=jnp.bfloat16):
    drawn = deviation * jax.random.normal(key, shape, jnp.float32)
    if cuts:
        drawn = drawn * block_levels(key, shape, cuts, -0.22, 0.18)
    return jnp.clip(drawn, -reach, reach).astype(held_as)


def setup_inputs(seed: int = 0) -> dict:
    key_of = jax.random.split(jax.random.key(seed), 7)
    return {
        "queries": draw_queries(jax.random.fold_in(key_of[6], 71), 0),
        "stretch_kv": draw_stretch_kv(jax.random.fold_in(key_of[6], 71), 0),
        "pool_kv": centred(key_of[2], (OWNERS * SLOTS, BLK, KVH, 2 * HD), 1.0, 6.0, ((0, 64), (2, 8))),
        "prefix_blocks": draw_prefix_blocks(jax.random.fold_in(key_of[6], 71), 0),
        "block_owner": draw_block_owner(jax.random.fold_in(key_of[6], 71), 0),
        "block_slot": set_ends(jax.random.randint(key_of[5], (REQS, MAXB), 0, SLOTS), jax.random.fold_in(key_of[5], 1), 0, SLOTS - 1).astype(jnp.int32),
    }


MASKED_SCORE = -1e+30

def reference(queries, stretch_kv, pool_kv, prefix_blocks, block_owner, block_slot):
    group_size = QH // KVH
    score_scale = 1.0 / math.sqrt(HD)
    pool_rows = (block_owner * SLOTS + block_slot).astype(jnp.int32)
    prefix_len = MAXB * BLK

    def per_request(request):
        query = queries[request].astype(jnp.float32).reshape(STRETCH, KVH, group_size, HD)
        prefix = jnp.take(pool_kv, pool_rows[request], axis=0).reshape(prefix_len, KVH, 2 * HD)
        keys_all = jnp.concatenate([prefix, stretch_kv[request]], axis=0).astype(jnp.float32)
        position = jnp.arange(prefix_len + STRETCH, dtype=jnp.int32)
        token = jnp.arange(STRETCH, dtype=jnp.int32)
        prefix_live = position < prefix_blocks[request] * BLK
        causal = position[None, :] - prefix_len <= token[:, None]
        usable = jnp.where(position[None, :] < prefix_len, prefix_live[None, :], causal)
        key_mask = usable[:, None, None, :]
        scores = jnp.einsum('tkgd,skd->tkgs', query, keys_all[..., :HD]) * score_scale
        scores = jnp.where(key_mask, scores, MASKED_SCORE)
        row_max = lax.optimization_barrier(jnp.max(scores, axis=-1, keepdims=True))
        weights = jnp.where(key_mask, jnp.exp(scores - row_max), 0.0)
        row_total = lax.optimization_barrier(jnp.sum(weights, axis=-1))
        rounded = lax.optimization_barrier(weights.astype(jnp.bfloat16)).astype(jnp.float32)
        output = jnp.einsum('tkgs,skd->tkgd', rounded, keys_all[..., HD:]) / row_total[..., None]
        return output.reshape(STRETCH, QH * HD).astype(jnp.bfloat16)
    return lax.map(per_request, jnp.arange(REQS).astype(jnp.int32))
```

```python
import functools
import math

import jax
import jax.numpy as jnp
from jax import lax
from jax.experimental import pallas as pl
from jax.experimental.pallas import tpu as pltpu
from jax.sharding import Mesh
from jax.sharding import PartitionSpec as P

QH = 64
KVH = 8
GROUP = QH // KVH
MASKED_SCORE = -1e30
PLANE = ("pool", "core")


def pick_kernel(plans, place, table, *refs):
    buffers, (out, sem) = refs[:-2], refs[-2:]
    x, z, c = place[0], place[1], place[2]
    pools, planes, cores = place[3], place[4], place[5]
    way = 1 - 2 * c
    copies = []
    for buffer, request_step, owner_step, column in plans:
        for peer in range(out.shape[0]):
            if request_step is None:
                slot = peer
            else:
                request_z = lax.rem(z + request_step * way + planes, planes)
                owner_z = lax.rem(z + owner_step * way + planes, planes)
                request = (peer // 2 * planes + request_z) * cores + peer % 2
                owner = (x * planes + owner_z) * cores + c
                slot = jnp.maximum(table[request, owner] - 1, 0)
            copy = pltpu.make_async_copy(buffers[buffer].at[slot], out.at[peer, column], sem)
            copy.start()
            copies.append(copy)
    for copy in copies:
        copy.wait()


def pick(place, table, buffers, plans, peers):
    block = buffers[0].shape[1:]
    columns = len(plans)
    return pl.pallas_call(
        functools.partial(pick_kernel, plans),
        grid_spec=pltpu.PrefetchScalarGridSpec(
            num_scalar_prefetch=2,
            grid=(1,),
            in_specs=[pl.BlockSpec(memory_space=pl.ANY)] * len(buffers),
            out_specs=pl.BlockSpec((peers, columns) + block, lambda *_: (0, 0, 0, 0)),
            scratch_shapes=[pltpu.SemaphoreType.DMA],
        ),
        out_shape=jax.ShapeDtypeStruct((peers, columns) + block, buffers[0].dtype),
    )(place, table, *buffers)


def attend_kernel(rounds, chunk, first, last, scale, place, table, *refs):
    refs = list(refs)
    q_ref = refs.pop(0)
    arrived = [refs.pop(0) for _ in rounds]
    if not first:
        acc_in, ml_in = refs.pop(0), refs.pop(0)
    if last:
        out_ref = refs.pop(0)
    else:
        acc_out, ml_out = refs.pop(0), refs.pop(0)
    turned = refs.pop(0) if first else q_ref
    blocks, acc, ml, sem = refs
    if not last:
        acc, ml = acc_out, ml_out
    x, z, c = place[0], place[1], place[2]
    planes, cores = place[4], place[5]
    me = (x * planes + z) * cores + c
    group, head_dim, tokens = acc.shape
    block_len = arrived[0].shape[2]

    def fetch(source, at):
        return pltpu.make_async_copy(source, blocks.at[pl.ds(at * block_len, block_len)], sem)

    count = jnp.int32(0)
    for array, steps in zip(arrived, rounds):
        for lane in range(array.shape[0]):
            way = 1 - 2 * (lane % 2)
            for column in range(array.shape[1]):
                owner_z = lax.rem(z + steps[column] * way + planes, planes)
                live = table[me, (lane // 2 * planes + owner_z) * cores + lane % 2] > 0

                @pl.when(live)
                def _():
                    fetch(array.at[lane, column], count).start()

                count = count + live.astype(jnp.int32)
    chunks = (count + chunk - 1) // chunk
    spare = arrived[0].at[0, 0]

    def fill(at, carried):
        fetch(spare, at).start()
        return carried

    def drain(at, carried):
        fetch(spare, at).wait()
        return carried

    lax.fori_loop(count, chunks * chunk, fill, 0)

    def scores_of(head, keys):
        query = turned[head * head_dim : (head + 1) * head_dim, :]
        return jnp.dot(keys, query, preferred_element_type=jnp.float32)

    def absorb(pending):
        head, weights, values, shrink = pending
        add = jnp.dot(values, weights, preferred_element_type=jnp.float32)
        acc[head] = add if shrink is None else acc[head] * shrink + add

    def sweep(keys, values, mask, fresh):
        score, pending = scores_of(0, keys), None
        for head in range(group):
            ahead = scores_of(head + 1, keys) if head + 1 < group else None
            score = mask(score)
            top = jnp.max(score, axis=0, keepdims=True)
            shrink = None
            if not fresh:
                old = ml[0, head : head + 1, :]
                top = jnp.maximum(top, old)
                shrink = jnp.exp2((old - top) * scale)
            weights = jnp.exp2((score - top) * scale)
            total = jnp.sum(weights, axis=0, keepdims=True)
            ml[1, head : head + 1, :] = total if fresh else ml[1, head : head + 1, :] * shrink + total
            ml[0, head : head + 1, :] = top
            if pending is not None:
                absorb(pending)
            pending = (head, weights.astype(values.dtype), values, shrink)
            score = ahead
        absorb(pending)

    if first:
        turned[...] = q_ref[:, : group * head_dim].T
        own = q_ref[:, group * head_dim :]
        key = lax.broadcasted_iota(jnp.int32, (tokens, tokens), 0)
        token = lax.broadcasted_iota(jnp.int32, (tokens, tokens), 1)
        sweep(own[:, :head_dim], own[:, head_dim:].T, lambda s: jnp.where(key <= token, s, MASKED_SCORE), True)
    else:
        acc[...] = acc_in[...]
        ml[...] = ml_in[...]
    lax.fori_loop(0, chunks * chunk, drain, 0)

    def body(at, carried):
        size = chunk * block_len
        kv = blocks[pl.ds(pl.multiple_of(at * size, size), size), :]

        def mask(score):
            parts = [score[:block_len]]
            for b in range(1, chunk):
                part = score[b * block_len : (b + 1) * block_len]
                parts.append(jnp.where(at * chunk + b < count, part, MASKED_SCORE))
            return jnp.concatenate(parts, axis=0)

        sweep(kv[:, :head_dim], kv[:, head_dim:].T, mask, False)
        return carried

    lax.fori_loop(0, chunks, body, 0)
    if last:
        for head in range(group):
            done = acc[head] / ml[1, head : head + 1, :]
            out_ref[:, head * head_dim : (head + 1) * head_dim] = done.T.astype(out_ref.dtype)


def attend(place, table, query, arrived, rounds, state, last, scale, group, head_dim, tokens, chunk=8):
    first = state is None
    dtype = arrived[0].dtype
    slots = sum(array.shape[0] * array.shape[1] for array in arrived)
    slots = (slots + chunk - 1) // chunk * chunk
    block_len = arrived[0].shape[2]
    whole = pl.BlockSpec(memory_space=pltpu.VMEM)
    operands = [query] + list(arrived) + ([] if first else list(state))
    in_specs = [whole] + [pl.BlockSpec(memory_space=pl.ANY)] * len(arrived) + ([] if first else [whole] * 2)
    acc = ((group, head_dim, tokens), jnp.float32)
    ml = ((2, group, tokens), jnp.float32)
    outs = [((tokens, group * head_dim), dtype)] if last else [acc, ml]
    if first:
        outs.append(((group * head_dim, tokens), dtype))
    return pl.pallas_call(
        functools.partial(attend_kernel, rounds, chunk, first, last, scale * math.log2(math.e)),
        grid_spec=pltpu.PrefetchScalarGridSpec(
            num_scalar_prefetch=2,
            grid=(1,),
            in_specs=in_specs,
            out_specs=[whole] * len(outs),
            scratch_shapes=[
                pltpu.VMEM((slots * block_len, 2 * head_dim), dtype),
                pltpu.VMEM(*acc),
                pltpu.VMEM(*ml),
                pltpu.SemaphoreType.DMA,
            ],
        ),
        out_shape=[jax.ShapeDtypeStruct(*out) for out in outs],
        compiler_params=pltpu.CompilerParams(vmem_limit_bytes=48 * 1024 * 1024),
    )(place, table, query, *operands[1:])


def local(queries, stretch_kv, pool_kv, prefix_blocks, block_owner, block_slot):
    pools, planes, cores = lax.axis_size("pool"), lax.axis_size("z"), lax.axis_size("core")
    x, z, c = lax.axis_index("pool"), lax.axis_index("z"), lax.axis_index("core")
    tensor_count = lax.axis_size("tp")
    owner_count = pools * planes * cores
    peers = pools * cores
    tok_local = queries.shape[1]
    block_len, pair = pool_kv.shape[1], pool_kv.shape[3]
    head_dim = pair // 2
    scale = 1.0 / math.sqrt(head_dim)
    max_blocks = block_owner.shape[1]
    pool = pool_kv.reshape(-1, block_len, pair)

    def hop(array, long):
        pairs = []
        for at in range(planes):
            for core in range(cores):
                way = (1 if core == 0 else -1) * (1 if long else -1)
                pairs.append((at * cores + core, (at + way) % planes * cores + core))
        return lax.ppermute(array, ("z", "core"), pairs)

    def deliver(array):
        return lax.all_to_all(array, PLANE, split_axis=0, concat_axis=0, tiled=True)

    long1, short1 = hop(pool, True), hop(pool, False)

    place = jnp.stack([x, z, c, jnp.int32(pools), jnp.int32(planes), jnp.int32(cores)]).astype(jnp.int32)
    position = jnp.arange(max_blocks, dtype=jnp.int32)
    live = position[None, :] < prefix_blocks[:, None]
    owners = jnp.arange(owner_count, dtype=jnp.int32)
    table = jnp.sum(
        jnp.where(
            (block_owner[:, :, None] == owners[None, None, :]) & live[:, :, None],
            block_slot[:, :, None] + 1,
            0,
        ),
        axis=1,
    )

    both = jnp.concatenate([queries[0].reshape(tok_local, tensor_count, -1), stretch_kv[0]], axis=2)
    q_kv = lax.all_to_all(both, "tp", split_axis=1, concat_axis=0, tiled=True)
    q_kv = q_kv.reshape(tok_local * tensor_count, -1)

    tokens = q_kv.shape[0]
    get = functools.partial(pick, place, table, peers=peers)
    step = functools.partial(
        attend, place, table, scale=scale, group=GROUP, head_dim=head_dim, tokens=tokens
    )
    half = planes // 2
    longs, shorts = [pool, long1], [pool, short1]
    waiting, rounds = [deliver(get([pool], ((0, 0, 0, 0),)))], [(0,)]
    query, state = q_kv, None
    for k in range(1, half):
        if k + 1 < half:
            longs.append(hop(longs[k], True))
        else:
            longs.append(hop(get([longs[k]], ((0, 1, -k, 0),)), True))
        if k + 1 < half - 1:
            shorts.append(hop(shorts[k], False))
        elif k + 1 == half - 1:
            shorts.append(hop(get([shorts[k]], ((0, -1, k, 0),)), False))
        source, short = longs[k], shorts[k]
        if k > 1:
            made = step(query, waiting, tuple(rounds), state, False)
            if state is None:
                query = made[2]
            state = made[:2]
            waiting, rounds = [arriving], [arriving_round]
            source, short, *state = lax.optimization_barrier((source, short, *state))
        if k < half - 1:
            out = get([source, short], ((0, 0, -k, 0), (1, 0, k, 1)))
        else:
            short = short.reshape((peers,) + short.shape[2:])
            out = get([source, short], ((0, 0, -k, 0), (1, None, None, 1)))
        arriving, arriving_round = deliver(out), (-k, k)
    waiting, rounds = waiting + [arriving], rounds + [arriving_round]
    final = deliver(longs[half])
    *state, = step(query, waiting, tuple(rounds), state, False)
    (attended,) = step(query, [final], ((-half,),), state, True)
    attended = attended.reshape(tensor_count, tok_local, -1)
    attended = lax.all_to_all(attended, "tp", split_axis=0, concat_axis=2, tiled=True)
    return attended


def solution(mesh):
    pools, seq, tensor = mesh.devices.shape
    fine = Mesh(mesh.devices.reshape(pools, seq // 2, 2, tensor), ("pool", "z", "core", "tp"))
    rows = ("pool", "z", "core")
    return jax.shard_map(
        local,
        mesh=fine,
        in_specs=(
            P(rows, "tp", None),
            P(rows, "tp", None, None),
            P(rows, None, "tp", None),
            P(),
            P(),
            P(),
        ),
        out_specs=P(rows, "tp", None),
        check_vma=False,
    )
```

```python
import functools
import math

import jax
import jax.numpy as jnp
from jax import lax
from jax.experimental import pallas as pl
from jax.experimental.pallas import tpu as pltpu
from jax.sharding import Mesh
from jax.sharding import PartitionSpec as P

QH = 64
KVH = 8
GROUP = QH // KVH
MASKED_SCORE = -1e30
PEERS = 8
PLANE = ("core", "pool")
ANY = pl.BlockSpec(memory_space=pltpu.HBM)
VMEM = pl.BlockSpec(memory_space=pltpu.VMEM)


def cost_of(microseconds):
    return pl.CostEstimate(
        flops=int(microseconds * 1.1e9), transcendentals=0, bytes_accessed=int(microseconds * 3.6e6)
    )


def pick_kernel(outputs, count, place, table, *refs):
    buffers, outs, sem = refs[:count], refs[-1 - len(outputs) : -1], refs[-1]
    x, z, c = place[0], place[1], place[2]
    planes, cores = place[4], place[5]
    way = 1 - 2 * c
    copies = []
    for out, columns in zip(outs, outputs):
        peers = out.shape[0]
        pools = peers // 2
        for column, (buffer, request_step, owner_step) in enumerate(columns):
            request_z = lax.rem(z + request_step * way + planes, planes)
            owner_z = lax.rem(z + owner_step * way + planes, planes)
            owner = (x * planes + owner_z) * cores + c
            for peer in range(peers):
                request = (peer % pools * planes + request_z) * cores + peer // pools
                slot = jnp.maximum(table[request, owner] - 1, 0)
                copy = pltpu.make_async_copy(buffers[buffer].at[slot], out.at[peer, column], sem)
                copy.start()
                copies.append(copy)
    for copy in copies:
        copy.wait()


def pick(place, table, buffers, outputs, peers, after=(), cost=4):
    block, dtype = buffers[0].shape[1:], buffers[0].dtype
    operands = list(buffers) + list(after)
    return pl.pallas_call(
        functools.partial(pick_kernel, outputs, len(buffers)),
        grid_spec=pltpu.PrefetchScalarGridSpec(
            num_scalar_prefetch=2,
            grid=(1,),
            in_specs=[ANY] * len(operands),
            out_specs=[pl.BlockSpec((peers, len(columns)) + block, lambda *_: (0, 0, 0, 0)) for columns in outputs],
            scratch_shapes=[pltpu.SemaphoreType.DMA],
        ),
        out_shape=[jax.ShapeDtypeStruct((peers, len(columns)) + block, dtype) for columns in outputs],
        cost_estimate=cost_of(cost),
    )(place, table, *operands)


def join_kernel(*refs):
    arrays, out, sem = refs[:-2], refs[-2], refs[-1]
    copies = [pltpu.make_async_copy(array, out.at[:, at : at + 1], sem) for at, array in enumerate(arrays)]
    for copy in copies:
        copy.start()
    for copy in copies:
        copy.wait()


def join(arrays, cost):
    peers, _, *block = arrays[0].shape
    shape = (peers, len(arrays), *block)
    return pl.pallas_call(
        join_kernel,
        grid=(1,),
        in_specs=[ANY] * len(arrays),
        out_specs=pl.BlockSpec(shape, lambda _: (0, 0, 0, 0)),
        scratch_shapes=[pltpu.SemaphoreType.DMA],
        out_shape=jax.ShapeDtypeStruct(shape, arrays[0].dtype),
        cost_estimate=cost_of(cost),
    )(*arrays)


def attend_kernel(rounds, chunk, first, last, scale, spare_operands, place, table, *refs):
    refs = list(refs)
    q_in = refs.pop(0)
    arrived = [refs.pop(0) for _ in rounds]
    if not first:
        acc_in, ml_in = refs.pop(0), refs.pop(0)
    del refs[:spare_operands]
    if last:
        out_ref = refs.pop(0)
    else:
        acc_out, ml_out = refs.pop(0), refs.pop(0)
    if first:
        turned_out = refs.pop(0)
    blocks, acc, ml, query_buffer, turned, sem, state_sem = refs
    x, z, c = place[0], place[1], place[2]
    pools, planes, cores = place[3], place[4], place[5]
    me = (x * planes + z) * cores + c
    group, head_dim, tokens = acc.shape
    block_len = arrived[0].shape[2]
    if first:
        loads = [pltpu.make_async_copy(q_in, query_buffer, state_sem)]
    else:
        pairs = ((q_in, turned), (acc_in, acc), (ml_in, ml))
        loads = [pltpu.make_async_copy(source, target, state_sem) for source, target in pairs]
    for load in loads:
        load.start()

    def fetch(source, at):
        return pltpu.make_async_copy(source, blocks.at[pl.ds(at * block_len, block_len)], sem)

    count = jnp.int32(0)
    for array, (start, steps) in zip(arrived, rounds):
        for lane in range(array.shape[0]):
            core, sender = divmod(start + lane, PEERS // 2)
            way = 1 - 2 * core
            for column in range(array.shape[1]):
                if steps[column] is None:
                    continue
                owner_z = lax.rem(z + steps[column] * way + planes, planes)
                live = table[me, (sender * planes + owner_z) * cores + core] > 0

                @pl.when(live)
                def _():
                    fetch(array.at[lane, column], count).start()

                count = count + live.astype(jnp.int32)
    chunks = (count + chunk - 1) // chunk
    spare = arrived[0].at[0, 0]

    def fill(at, carried):
        fetch(spare, at).start()
        return carried

    def drain(at, carried):
        fetch(spare, at).wait()
        return carried

    lax.fori_loop(count, chunks * chunk, fill, 0)

    def scores_of(head, keys):
        query = turned[head * head_dim : (head + 1) * head_dim, :]
        return jnp.dot(keys, query, preferred_element_type=jnp.float32)

    def absorb(pending):
        head, weights, values, shrink = pending
        add = jnp.dot(values, weights, preferred_element_type=jnp.float32)
        acc[head] = add if shrink is None else acc[head] * shrink + add

    def sweep(keys, values, mask, fresh):
        score, pending = scores_of(0, keys), None
        for head in range(group):
            ahead = scores_of(head + 1, keys) if head + 1 < group else None
            score = mask(score)
            top = jnp.max(score, axis=0, keepdims=True)
            shrink = None
            if not fresh:
                old = ml[0, head : head + 1, :]
                top = jnp.maximum(top, old)
                shrink = jnp.exp2((old - top) * scale)
            weights = jnp.exp2((score - top) * scale)
            total = jnp.sum(weights, axis=0, keepdims=True)
            ml[1, head : head + 1, :] = total if fresh else ml[1, head : head + 1, :] * shrink + total
            ml[0, head : head + 1, :] = top
            if pending is not None:
                absorb(pending)
            pending = (head, weights.astype(values.dtype), values, shrink)
            score = ahead
        absorb(pending)

    for load in loads:
        load.wait()
    if first:
        turned[...] = query_buffer[:, : group * head_dim].T
        own = query_buffer[:, group * head_dim :]
        key = lax.broadcasted_iota(jnp.int32, (tokens, tokens), 0)
        token = lax.broadcasted_iota(jnp.int32, (tokens, tokens), 1)
        sweep(own[:, :head_dim], own[:, head_dim:].T, lambda s: jnp.where(key <= token, s, MASKED_SCORE), True)
    lax.fori_loop(0, chunks * chunk, drain, 0)

    def body(at, carried):
        size = chunk * block_len
        kv = blocks[pl.ds(pl.multiple_of(at * size, size), size), :]

        def mask(score):
            parts = [score[:block_len]]
            for b in range(1, chunk):
                part = score[b * block_len : (b + 1) * block_len]
                parts.append(jnp.where(at * chunk + b < count, part, MASKED_SCORE))
            return jnp.concatenate(parts, axis=0)

        sweep(kv[:, :head_dim], kv[:, head_dim:].T, mask, False)
        return carried

    lax.fori_loop(0, chunks, body, 0)
    if last:
        for head in range(group):
            done = acc[head] / ml[1, head : head + 1, :]
            out_ref[:, head * head_dim : (head + 1) * head_dim] = done.T.astype(out_ref.dtype)
    else:
        pairs = [(acc, acc_out), (ml, ml_out)] + ([(turned, turned_out)] if first else [])
        stores = [pltpu.make_async_copy(source, target, state_sem) for source, target in pairs]
        for store in stores:
            store.start()
        for store in stores:
            store.wait()


def attend(place, table, query, arrived, rounds, state, last, scale, group, head_dim, tokens, after=(), cost=8, chunk=8):
    first = state is None
    dtype = arrived[0].dtype
    slots = sum(array.shape[0] * array.shape[1] for array in arrived)
    slots = (slots + chunk - 1) // chunk * chunk
    block_len = arrived[0].shape[2]
    operands = [query] + list(arrived) + ([] if first else list(state)) + list(after)
    acc = ((group, head_dim, tokens), jnp.float32)
    ml = ((2, group, tokens), jnp.float32)
    turned = ((group * head_dim, tokens), dtype)
    outs = [((tokens, group * head_dim), dtype)] if last else [acc, ml]
    if first:
        outs.append(turned)
    return pl.pallas_call(
        functools.partial(
            attend_kernel, rounds, chunk, first, last, scale * math.log2(math.e), len(after)
        ),
        grid_spec=pltpu.PrefetchScalarGridSpec(
            num_scalar_prefetch=2,
            grid=(1,),
            in_specs=[ANY] * len(operands),
            out_specs=[VMEM if last else ANY] * len(outs),
            scratch_shapes=[
                pltpu.VMEM((slots * block_len, 2 * head_dim), dtype),
                pltpu.VMEM(*acc),
                pltpu.VMEM(*ml),
                pltpu.VMEM(query.shape if first else (16, 128), dtype),
                pltpu.VMEM(*turned),
                pltpu.SemaphoreType.DMA,
                pltpu.SemaphoreType.DMA,
            ],
        ),
        out_shape=[jax.ShapeDtypeStruct(*out) for out in outs],
        compiler_params=pltpu.CompilerParams(vmem_limit_bytes=20 * 1024 * 1024),
        cost_estimate=cost_of(cost),
    )(place, table, *operands)


def local(queries, stretch_kv, pool_kv, prefix_blocks, block_owner, block_slot):
    pools, planes, cores = lax.axis_size("pool"), lax.axis_size("z"), lax.axis_size("core")
    x, z, c = lax.axis_index("pool"), lax.axis_index("z"), lax.axis_index("core")
    tensor_count = lax.axis_size("tp")
    owner_count = pools * planes * cores
    peers = pools * cores
    tok_local = queries.shape[1]
    block_len, pair = pool_kv.shape[1], pool_kv.shape[3]
    head_dim = pair // 2
    scale = 1.0 / math.sqrt(head_dim)
    max_blocks = block_owner.shape[1]
    pool = pool_kv.reshape(-1, block_len, pair)

    def hop(array, step, mirrored):
        pairs = []
        for at in range(planes):
            for core in range(cores):
                way = -step if mirrored and core else step
                pairs.append((at * cores + core, (at + way) % planes * cores + core))
        return lax.ppermute(array, ("z", "core"), pairs)

    def deliver(array):
        return lax.all_to_all(array, PLANE, split_axis=0, concat_axis=0, tiled=True)

    long1, short1 = hop(pool, 1, True), hop(pool, -1, True)

    where = (x, z, c, pools, planes, cores)
    place = jnp.stack([jnp.int32(value) for value in where])
    position = jnp.arange(max_blocks, dtype=jnp.int32)
    live = position[None, :] < prefix_blocks[:, None]
    owners = jnp.arange(owner_count, dtype=jnp.int32)
    table = jnp.sum(
        jnp.where(
            (block_owner[:, :, None] == owners[None, None, :]) & live[:, :, None],
            block_slot[:, :, None] + 1,
            0,
        ),
        axis=1,
    )

    both = jnp.concatenate([queries[0].reshape(tok_local, tensor_count, -1), stretch_kv[0]], axis=2)
    q_kv = lax.all_to_all(both, "tp", split_axis=1, concat_axis=0, tiled=True)
    tokens = tok_local * tensor_count
    q_kv = q_kv.reshape(tokens, -1)
    get = functools.partial(pick, place, table, peers=peers)
    step = functools.partial(
        attend, place, table, scale=scale, group=GROUP, head_dim=head_dim, tokens=tokens
    )
    long2, short2 = hop(long1, 1, True), hop(short1, -1, True)
    half_peers = peers // 2
    (start,) = get([pool], (((0, 4, 0), (0, 0, 0)),))
    start, q_kv = lax.optimization_barrier((start, q_kv))
    start = deliver(start)
    (send_near,) = get([long1, short1], (((0, 0, -1), (1, 0, 1)),))
    near = deliver(send_near)
    *state, query = step(q_kv, [start], ((0, (None, 0)),), None, False, after=[send_near])
    send_long, send_short = get([long2, short2], (((0, 1, -2),), ((1, -1, 2),)), after=[state[0]])
    long3, short3 = hop(send_long, 1, True), hop(send_short, -1, True)
    (middle_sent,) = get([long2, short2], (((0, 0, -2), (1, 0, 2)),), after=[send_long])
    middle = deliver(middle_sent)
    state = step(query, [near], ((0, (-1, 1)),), state, False, after=[middle_sent])
    far, long3 = lax.optimization_barrier((start, long3))
    far_up, far_down = hop(far[:half_peers, :1], 4, False), hop(far[half_peers:, :1], -4, False)
    third = join([long3, short3], cost=30)
    state = step(query, [middle], ((0, (-2, 2)),), state, False, after=[third], cost=10)
    third = deliver(third)
    (attended,) = step(
        query, [third, far_up, far_down], ((0, (-3, 3)), (0, (4,)), (half_peers, (4,))), state, True
    )
    attended = attended.reshape(tensor_count, tok_local, -1)
    return lax.all_to_all(attended, "tp", split_axis=0, concat_axis=2, tiled=True)


def solution(mesh):
    pools, seq, tensor = mesh.devices.shape
    fine = Mesh(mesh.devices.reshape(pools, seq // 2, 2, tensor), ("pool", "z", "core", "tp"))
    rows = ("pool", "z", "core")
    return jax.shard_map(
        local,
        mesh=fine,
        in_specs=(
            P(rows, "tp", None),
            P(rows, "tp", None, None),
            P(rows, None, "tp", None),
            P(),
            P(),
            P(),
        ),
        out_specs=P(rows, "tp", None),
        check_vma=False,
    )
```

```python
import functools
import math

import jax
import jax.numpy as jnp
from jax import lax
from jax.experimental import pallas as pl
from jax.experimental.pallas import tpu as pltpu
from jax.sharding import Mesh
from jax.sharding import PartitionSpec as P

QH = 64
KVH = 8
GROUP = QH // KVH
MASKED_SCORE = -1e30
PEERS = 8
PLANE = ("core", "pool")
ANY = pl.BlockSpec(memory_space=pltpu.HBM)
VMEM = pl.BlockSpec(memory_space=pltpu.VMEM)


def cost_of(microseconds):
    return pl.CostEstimate(
        flops=int(microseconds * 1.1e9), transcendentals=0, bytes_accessed=int(microseconds * 3.6e6)
    )


def pick_kernel(outputs, count, place, table, *refs):
    buffers, outs, sem = refs[:count], refs[-1 - len(outputs) : -1], refs[-1]
    x, z, c = place[0], place[1], place[2]
    planes, cores = place[4], place[5]
    way = 1 - 2 * c
    copies = []
    for out, columns in zip(outs, outputs):
        peers = out.shape[0]
        pools = peers // 2
        for column, (buffer, request_step, owner_step) in enumerate(columns):
            request_z = lax.rem(z + request_step * way + planes, planes)
            owner_z = lax.rem(z + owner_step * way + planes, planes)
            owner = (x * planes + owner_z) * cores + c
            for peer in range(peers):
                request = (peer % pools * planes + request_z) * cores + peer // pools
                slot = jnp.maximum(table[request, owner] - 1, 0)
                copy = pltpu.make_async_copy(buffers[buffer].at[slot], out.at[peer, column], sem)
                copy.start()
                copies.append(copy)
    for copy in copies:
        copy.wait()


def pick(place, table, buffers, outputs, peers, after=(), cost=4):
    block, dtype = buffers[0].shape[1:], buffers[0].dtype
    operands = list(buffers) + list(after)
    return pl.pallas_call(
        functools.partial(pick_kernel, outputs, len(buffers)),
        grid_spec=pltpu.PrefetchScalarGridSpec(
            num_scalar_prefetch=2,
            grid=(1,),
            in_specs=[ANY] * len(operands),
            out_specs=[pl.BlockSpec((peers, len(columns)) + block, lambda *_: (0, 0, 0, 0)) for columns in outputs],
            scratch_shapes=[pltpu.SemaphoreType.DMA],
        ),
        out_shape=[jax.ShapeDtypeStruct((peers, len(columns)) + block, dtype) for columns in outputs],
        cost_estimate=cost_of(cost),
    )(place, table, *operands)


def join_kernel(*refs):
    arrays, out, sem = refs[:-2], refs[-2], refs[-1]
    copies = [pltpu.make_async_copy(array, out.at[:, at : at + 1], sem) for at, array in enumerate(arrays)]
    for copy in copies:
        copy.start()
    for copy in copies:
        copy.wait()


def join(arrays, cost):
    peers, _, *block = arrays[0].shape
    shape = (peers, len(arrays), *block)
    return pl.pallas_call(
        join_kernel,
        grid=(1,),
        in_specs=[ANY] * len(arrays),
        out_specs=pl.BlockSpec(shape, lambda _: (0, 0, 0, 0)),
        scratch_shapes=[pltpu.SemaphoreType.DMA],
        out_shape=jax.ShapeDtypeStruct(shape, arrays[0].dtype),
        cost_estimate=cost_of(cost),
    )(*arrays)


def attend_kernel(rounds, chunk, first, last, scale, spare_operands, place, table, *refs):
    refs = list(refs)
    q_in = refs.pop(0)
    arrived = [refs.pop(0) for _ in rounds]
    if not first:
        acc_in, ml_in = refs.pop(0), refs.pop(0)
    del refs[:spare_operands]
    if last:
        out_ref = refs.pop(0)
    else:
        acc_out, ml_out = refs.pop(0), refs.pop(0)
    if first:
        turned_out = refs.pop(0)
    blocks, acc, ml, query_buffer, turned, sem, state_sem = refs
    x, z, c = place[0], place[1], place[2]
    pools, planes, cores = place[3], place[4], place[5]
    me = (x * planes + z) * cores + c
    group, head_dim, tokens = acc.shape
    block_len = arrived[0].shape[2]
    if first:
        loads = [pltpu.make_async_copy(q_in, query_buffer, state_sem)]
    else:
        pairs = ((q_in, turned), (acc_in, acc), (ml_in, ml))
        loads = [pltpu.make_async_copy(source, target, state_sem) for source, target in pairs]
    for load in loads:
        load.start()

    def fetch(source, at):
        return pltpu.make_async_copy(source, blocks.at[pl.ds(at * block_len, block_len)], sem)

    count = jnp.int32(0)
    for array, (start, steps) in zip(arrived, rounds):
        for lane in range(array.shape[0]):
            core, sender = divmod(start + lane, PEERS // 2)
            way = 1 - 2 * core
            for column in range(array.shape[1]):
                if steps[column] is None:
                    continue
                owner_z = lax.rem(z + steps[column] * way + planes, planes)
                live = table[me, (sender * planes + owner_z) * cores + core] > 0

                @pl.when(live)
                def _():
                    fetch(array.at[lane, column], count).start()

                count = count + live.astype(jnp.int32)
    chunks = (count + chunk - 1) // chunk
    spare = arrived[0].at[0, 0]

    def fill(at, carried):
        fetch(spare, at).start()
        return carried

    def drain(at, carried):
        fetch(spare, at).wait()
        return carried

    lax.fori_loop(count, chunks * chunk, fill, 0)

    def scores_of(head, keys):
        query = turned[head * head_dim : (head + 1) * head_dim, :]
        return jnp.dot(keys, query, preferred_element_type=jnp.float32)

    def absorb(pending):
        head, weights, values, shrink = pending
        add = jnp.dot(values, weights, preferred_element_type=jnp.float32)
        acc[head] = add if shrink is None else acc[head] * shrink + add

    def sweep(keys, values, mask, fresh):
        score, pending = scores_of(0, keys), None
        for head in range(group):
            ahead = scores_of(head + 1, keys) if head + 1 < group else None
            score = mask(score)
            top = jnp.max(score, axis=0, keepdims=True)
            shrink = None
            if not fresh:
                old = ml[0, head : head + 1, :]
                top = jnp.maximum(top, old)
                shrink = jnp.exp2((old - top) * scale)
            weights = jnp.exp2((score - top) * scale)
            total = jnp.sum(weights, axis=0, keepdims=True)
            ml[1, head : head + 1, :] = total if fresh else ml[1, head : head + 1, :] * shrink + total
            ml[0, head : head + 1, :] = top
            if pending is not None:
                absorb(pending)
            pending = (head, weights.astype(values.dtype), values, shrink)
            score = ahead
        absorb(pending)

    for load in loads:
        load.wait()
    if first:
        turned[...] = query_buffer[:, : group * head_dim].T
        own = query_buffer[:, group * head_dim :]
        key = lax.broadcasted_iota(jnp.int32, (tokens, tokens), 0)
        token = lax.broadcasted_iota(jnp.int32, (tokens, tokens), 1)
        sweep(own[:, :head_dim], own[:, head_dim:].T, lambda s: jnp.where(key <= token, s, MASKED_SCORE), True)
    lax.fori_loop(0, chunks * chunk, drain, 0)

    def body(at, carried):
        size = chunk * block_len
        kv = blocks[pl.ds(pl.multiple_of(at * size, size), size), :]

        def mask(score):
            parts = [score[:block_len]]
            for b in range(1, chunk):
                part = score[b * block_len : (b + 1) * block_len]
                parts.append(jnp.where(at * chunk + b < count, part, MASKED_SCORE))
            return jnp.concatenate(parts, axis=0)

        sweep(kv[:, :head_dim], kv[:, head_dim:].T, mask, False)
        return carried

    lax.fori_loop(0, chunks, body, 0)
    if last:
        for head in range(group):
            done = acc[head] / ml[1, head : head + 1, :]
            out_ref[:, head * head_dim : (head + 1) * head_dim] = done.T.astype(out_ref.dtype)
    else:
        pairs = [(acc, acc_out), (ml, ml_out)] + ([(turned, turned_out)] if first else [])
        stores = [pltpu.make_async_copy(source, target, state_sem) for source, target in pairs]
        for store in stores:
            store.start()
        for store in stores:
            store.wait()


def attend(place, table, query, arrived, rounds, state, last, scale, group, head_dim, tokens, after=(), cost=8, chunk=8):
    first = state is None
    dtype = arrived[0].dtype
    slots = sum(array.shape[0] * array.shape[1] for array in arrived)
    slots = (slots + chunk - 1) // chunk * chunk
    block_len = arrived[0].shape[2]
    operands = [query] + list(arrived) + ([] if first else list(state)) + list(after)
    acc = ((group, head_dim, tokens), jnp.float32)
    ml = ((2, group, tokens), jnp.float32)
    turned = ((group * head_dim, tokens), dtype)
    outs = [((tokens, group * head_dim), dtype)] if last else [acc, ml]
    if first:
        outs.append(turned)
    return pl.pallas_call(
        functools.partial(
            attend_kernel, rounds, chunk, first, last, scale * math.log2(math.e), len(after)
        ),
        grid_spec=pltpu.PrefetchScalarGridSpec(
            num_scalar_prefetch=2,
            grid=(1,),
            in_specs=[ANY] * len(operands),
            out_specs=[VMEM if last else ANY] * len(outs),
            scratch_shapes=[
                pltpu.VMEM((slots * block_len, 2 * head_dim), dtype),
                pltpu.VMEM(*acc),
                pltpu.VMEM(*ml),
                pltpu.VMEM(query.shape if first else (16, 128), dtype),
                pltpu.VMEM(*turned),
                pltpu.SemaphoreType.DMA,
                pltpu.SemaphoreType.DMA,
            ],
        ),
        out_shape=[jax.ShapeDtypeStruct(*out) for out in outs],
        compiler_params=pltpu.CompilerParams(vmem_limit_bytes=20 * 1024 * 1024),
        cost_estimate=cost_of(cost),
    )(place, table, *operands)


def local(queries, stretch_kv, pool_kv, prefix_blocks, block_owner, block_slot):
    pools, planes, cores = lax.axis_size("pool"), lax.axis_size("z"), lax.axis_size("core")
    x, z, c = lax.axis_index("pool"), lax.axis_index("z"), lax.axis_index("core")
    tensor_count = lax.axis_size("tp")
    owner_count = pools * planes * cores
    peers = pools * cores
    tok_local = queries.shape[1]
    block_len, pair = pool_kv.shape[1], pool_kv.shape[3]
    head_dim = pair // 2
    scale = 1.0 / math.sqrt(head_dim)
    max_blocks = block_owner.shape[1]
    pool = pool_kv.reshape(-1, block_len, pair)

    def hop(array, step, mirrored):
        pairs = []
        for at in range(planes):
            for core in range(cores):
                way = -step if mirrored and core else step
                pairs.append((at * cores + core, (at + way) % planes * cores + core))
        return lax.ppermute(array, ("z", "core"), pairs)

    def deliver(array):
        return lax.all_to_all(array, PLANE, split_axis=0, concat_axis=0, tiled=True)

    long1, short1 = hop(pool, 1, True), hop(pool, -1, True)

    where = (x, z, c, pools, planes, cores)
    place = jnp.stack([jnp.int32(value) for value in where])
    position = jnp.arange(max_blocks, dtype=jnp.int32)
    live = position[None, :] < prefix_blocks[:, None]
    owners = jnp.arange(owner_count, dtype=jnp.int32)
    table = jnp.sum(
        jnp.where(
            (block_owner[:, :, None] == owners[None, None, :]) & live[:, :, None],
            block_slot[:, :, None] + 1,
            0,
        ),
        axis=1,
    )

    both = jnp.concatenate([queries[0].reshape(tok_local, tensor_count, -1), stretch_kv[0]], axis=2)
    q_kv = lax.all_to_all(both, "tp", split_axis=1, concat_axis=0, tiled=True)
    tokens = tok_local * tensor_count
    q_kv = q_kv.reshape(tokens, -1)
    get = functools.partial(pick, place, table, peers=peers)
    step = functools.partial(
        attend, place, table, scale=scale, group=GROUP, head_dim=head_dim, tokens=tokens
    )
    long2, short2 = hop(long1, 1, True), hop(short1, -1, True)
    half_peers = peers // 2
    (start,) = get([pool], (((0, 4, 0), (0, 0, 0)),))
    start, q_kv = lax.optimization_barrier((start, q_kv))
    start = deliver(start)
    (send_near,) = get([long1, short1], (((0, 0, -1), (1, 0, 1)),))
    near = deliver(send_near)
    *state, query = step(q_kv, [start], ((0, (None, 0)),), None, False, after=[send_near])
    send_long, send_short, middle_sent = get(
        [long2, short2],
        (((0, 1, -2),), ((1, -1, 2),), ((0, 0, -2), (1, 0, 2))),
        after=[state[0]],
        cost=40,
    )
    far, _ = lax.optimization_barrier((start, near))
    long3, short3 = hop(send_long, 1, True), hop(send_short, -1, True)
    middle = deliver(middle_sent)
    far_up, far_down = hop(far[:half_peers, :1], 4, False), hop(far[half_peers:, :1], -4, False)
    third = join([long3, short3], cost=4)
    state = step(query, [near, middle], ((0, (-1, 1)), (0, (-2, 2))), state, False, after=[third], cost=60)
    third = deliver(third)
    (attended,) = step(
        query, [third, far_up, far_down], ((0, (-3, 3)), (0, (4,)), (half_peers, (4,))), state, True
    )
    attended = attended.reshape(tensor_count, tok_local, -1)
    return lax.all_to_all(attended, "tp", split_axis=0, concat_axis=2, tiled=True)


def solution(mesh):
    pools, seq, tensor = mesh.devices.shape
    fine = Mesh(mesh.devices.reshape(pools, seq // 2, 2, tensor), ("pool", "z", "core", "tp"))
    rows = ("pool", "z", "core")
    return jax.shard_map(
        local,
        mesh=fine,
        in_specs=(
            P(rows, "tp", None),
            P(rows, "tp", None, None),
            P(rows, None, "tp", None),
            P(),
            P(),
            P(),
        ),
        out_specs=P(rows, "tp", None),
        check_vma=False,
    )
```

```python
import functools
import math

import jax
import jax.numpy as jnp
from jax import lax
from jax.experimental import pallas as pl
from jax.experimental.pallas import tpu as pltpu
from jax.sharding import Mesh
from jax.sharding import PartitionSpec as P

QH = 64
KVH = 8
GROUP = QH // KVH
MASKED_SCORE = -1e30
PEERS = 8
PLANE = ("core", "pool")
ANY = pl.BlockSpec(memory_space=pltpu.HBM)
VMEM = pl.BlockSpec(memory_space=pltpu.VMEM)


def cost_of(microseconds):
    return pl.CostEstimate(
        flops=int(microseconds * 1.1e9), transcendentals=0, bytes_accessed=int(microseconds * 3.6e6)
    )


def pick_kernel(outputs, count, place, table, *refs):
    buffers, outs, sem = refs[:count], refs[-1 - len(outputs) : -1], refs[-1]
    x, z, c = place[0], place[1], place[2]
    planes, cores = place[4], place[5]
    way = 1 - 2 * c
    copies = []
    for out, columns in zip(outs, outputs):
        peers = out.shape[0]
        pools = peers // 2
        for column, (buffer, request_step, owner_step) in enumerate(columns):
            request_z = lax.rem(z + request_step * way + planes, planes)
            owner_z = lax.rem(z + owner_step * way + planes, planes)
            owner = (x * planes + owner_z) * cores + c
            for peer in range(peers):
                request = (peer % pools * planes + request_z) * cores + peer // pools
                slot = jnp.maximum(table[request, owner] - 1, 0)
                copy = pltpu.make_async_copy(buffers[buffer].at[slot], out.at[peer, column], sem)
                copy.start()
                copies.append(copy)
    for copy in copies:
        copy.wait()


def pick(place, table, buffers, outputs, peers, after=(), cost=4):
    block, dtype = buffers[0].shape[1:], buffers[0].dtype
    operands = list(buffers) + list(after)
    return pl.pallas_call(
        functools.partial(pick_kernel, outputs, len(buffers)),
        grid_spec=pltpu.PrefetchScalarGridSpec(
            num_scalar_prefetch=2,
            grid=(1,),
            in_specs=[ANY] * len(operands),
            out_specs=[pl.BlockSpec((peers, len(columns)) + block, lambda *_: (0, 0, 0, 0)) for columns in outputs],
            scratch_shapes=[pltpu.SemaphoreType.DMA],
        ),
        out_shape=[jax.ShapeDtypeStruct((peers, len(columns)) + block, dtype) for columns in outputs],
        cost_estimate=cost_of(cost),
    )(place, table, *operands)


def join_kernel(*refs):
    arrays, out, sem = refs[:-2], refs[-2], refs[-1]
    copies = [pltpu.make_async_copy(array, out.at[:, at : at + 1], sem) for at, array in enumerate(arrays)]
    for copy in copies:
        copy.start()
    for copy in copies:
        copy.wait()


def join(arrays, cost):
    peers, _, *block = arrays[0].shape
    shape = (peers, len(arrays), *block)
    return pl.pallas_call(
        join_kernel,
        grid=(1,),
        in_specs=[ANY] * len(arrays),
        out_specs=pl.BlockSpec(shape, lambda _: (0, 0, 0, 0)),
        scratch_shapes=[pltpu.SemaphoreType.DMA],
        out_shape=jax.ShapeDtypeStruct(shape, arrays[0].dtype),
        cost_estimate=cost_of(cost),
    )(*arrays)


def attend_kernel(rounds, chunk, first, last, scale, spare_operands, place, table, *refs):
    refs = list(refs)
    q_in = refs.pop(0)
    arrived = [refs.pop(0) for _ in rounds]
    if not first:
        acc_in, ml_in = refs.pop(0), refs.pop(0)
    del refs[:spare_operands]
    if last:
        out_ref = refs.pop(0)
    else:
        acc_out, ml_out = refs.pop(0), refs.pop(0)
    if first:
        turned_out = refs.pop(0)
    blocks, acc, ml, query_buffer, turned, sem, state_sem = refs
    x, z, c = place[0], place[1], place[2]
    pools, planes, cores = place[3], place[4], place[5]
    me = (x * planes + z) * cores + c
    group, head_dim, tokens = acc.shape
    block_len = arrived[0].shape[2]
    if first:
        loads = [pltpu.make_async_copy(q_in, query_buffer, state_sem)]
    else:
        pairs = ((q_in, turned), (acc_in, acc), (ml_in, ml))
        loads = [pltpu.make_async_copy(source, target, state_sem) for source, target in pairs]
    for load in loads:
        load.start()

    def fetch(source, at):
        return pltpu.make_async_copy(source, blocks.at[pl.ds(at * block_len, block_len)], sem)

    count = jnp.int32(0)
    for array, (start, steps) in zip(arrived, rounds):
        for lane in range(array.shape[0]):
            core, sender = divmod(start + lane, PEERS // 2)
            way = 1 - 2 * core
            for column in range(array.shape[1]):
                if steps[column] is None:
                    continue
                owner_z = lax.rem(z + steps[column] * way + planes, planes)
                live = table[me, (sender * planes + owner_z) * cores + core] > 0

                @pl.when(live)
                def _():
                    fetch(array.at[lane, column], count).start()

                count = count + live.astype(jnp.int32)
    half = chunk // 2
    wholes = (count + half - 1) // chunk
    halves = (jnp.maximum(count - wholes * chunk, 0) + half - 1) // half
    held = wholes * chunk + halves * half
    spare = arrived[0].at[0, 0]

    def fill(at, carried):
        fetch(spare, at).start()
        return carried

    def drain(at, carried):
        fetch(spare, at).wait()
        return carried

    lax.fori_loop(count, held, fill, 0)

    def scores_of(head, keys):
        query = turned[head * head_dim : (head + 1) * head_dim, :]
        return jnp.dot(keys, query, preferred_element_type=jnp.float32)

    def absorb(pending):
        head, weights, values, shrink = pending
        add = jnp.dot(values, weights, preferred_element_type=jnp.float32)
        acc[head] = add if shrink is None else acc[head] * shrink + add

    def sweep(keys, values, mask, fresh):
        score, pending = scores_of(0, keys), None
        for head in range(group):
            ahead = scores_of(head + 1, keys) if head + 1 < group else None
            score = mask(score)
            top = jnp.max(score, axis=0, keepdims=True)
            shrink = None
            if not fresh:
                old = ml[0, head : head + 1, :]
                top = jnp.maximum(top, old)
                shrink = jnp.exp2((old - top) * scale)
            weights = jnp.exp2((score - top) * scale)
            total = jnp.sum(weights, axis=0, keepdims=True)
            ml[1, head : head + 1, :] = total if fresh else ml[1, head : head + 1, :] * shrink + total
            ml[0, head : head + 1, :] = top
            if pending is not None:
                absorb(pending)
            pending = (head, weights.astype(values.dtype), values, shrink)
            score = ahead
        absorb(pending)

    for load in loads:
        load.wait()
    if first:
        turned[...] = query_buffer[:, : group * head_dim].T
        own = query_buffer[:, group * head_dim :]
        key = lax.broadcasted_iota(jnp.int32, (tokens, tokens), 0)
        token = lax.broadcasted_iota(jnp.int32, (tokens, tokens), 1)
        sweep(own[:, :head_dim], own[:, head_dim:].T, lambda s: jnp.where(key <= token, s, MASKED_SCORE), True)
    lax.fori_loop(0, held, drain, 0)

    def take(base, length, sure):
        size = length * block_len
        kv = blocks[pl.ds(pl.multiple_of(base * block_len, half * block_len), size), :]

        def mask(score):
            parts = [score[: sure * block_len]]
            for b in range(sure, length):
                part = score[b * block_len : (b + 1) * block_len]
                parts.append(jnp.where(base + b < count, part, MASKED_SCORE))
            return jnp.concatenate(parts, axis=0)

        sweep(kv[:, :head_dim], kv[:, head_dim:].T, mask, False)

    def body(at, carried):
        take(at * chunk, chunk, half + 1)
        return carried

    lax.fori_loop(0, wholes, body, 0)

    @pl.when(halves > 0)
    def _():
        take(wholes * chunk, half, 1)

    if last:
        for head in range(group):
            done = acc[head] / ml[1, head : head + 1, :]
            out_ref[:, head * head_dim : (head + 1) * head_dim] = done.T.astype(out_ref.dtype)
    else:
        pairs = [(acc, acc_out), (ml, ml_out)] + ([(turned, turned_out)] if first else [])
        stores = [pltpu.make_async_copy(source, target, state_sem) for source, target in pairs]
        for store in stores:
            store.start()
        for store in stores:
            store.wait()


def attend(place, table, query, arrived, rounds, state, last, scale, group, head_dim, tokens, after=(), cost=8, chunk=8):
    first = state is None
    dtype = arrived[0].dtype
    slots = sum(array.shape[0] * array.shape[1] for array in arrived)
    slots = (slots + chunk - 1) // chunk * chunk
    block_len = arrived[0].shape[2]
    operands = [query] + list(arrived) + ([] if first else list(state)) + list(after)
    kept = range(1) if first else (0, 1 + len(arrived), 2 + len(arrived))
    for at in kept:
        operands[at] = pltpu.with_memory_space_constraint(operands[at], pltpu.HBM)
    acc = ((group, head_dim, tokens), jnp.float32)
    ml = ((2, group, tokens), jnp.float32)
    turned = ((group * head_dim, tokens), dtype)
    outs = [((tokens, group * head_dim), dtype)] if last else [acc, ml]
    if first:
        outs.append(turned)
    return pl.pallas_call(
        functools.partial(
            attend_kernel, rounds, chunk, first, last, scale * math.log2(math.e), len(after)
        ),
        grid_spec=pltpu.PrefetchScalarGridSpec(
            num_scalar_prefetch=2,
            grid=(1,),
            in_specs=[ANY] * len(operands),
            out_specs=[VMEM if last else ANY] * len(outs),
            scratch_shapes=[
                pltpu.VMEM((slots * block_len, 2 * head_dim), dtype),
                pltpu.VMEM(*acc),
                pltpu.VMEM(*ml),
                pltpu.VMEM(query.shape if first else (16, 128), dtype),
                pltpu.VMEM(*turned),
                pltpu.SemaphoreType.DMA,
                pltpu.SemaphoreType.DMA,
            ],
        ),
        out_shape=[(jax.ShapeDtypeStruct if last else pltpu.HBM)(*out) for out in outs],
        compiler_params=pltpu.CompilerParams(vmem_limit_bytes=20 * 1024 * 1024),
        cost_estimate=cost_of(cost),
    )(place, table, *operands)


def local(queries, stretch_kv, pool_kv, prefix_blocks, block_owner, block_slot):
    pools, planes, cores = lax.axis_size("pool"), lax.axis_size("z"), lax.axis_size("core")
    x, z, c = lax.axis_index("pool"), lax.axis_index("z"), lax.axis_index("core")
    tensor_count = lax.axis_size("tp")
    owner_count = pools * planes * cores
    peers = pools * cores
    tok_local = queries.shape[1]
    block_len, pair = pool_kv.shape[1], pool_kv.shape[3]
    head_dim = pair // 2
    scale = 1.0 / math.sqrt(head_dim)
    max_blocks = block_owner.shape[1]
    pool = pool_kv.reshape(-1, block_len, pair)

    def hop(array, step, mirrored):
        pairs = []
        for at in range(planes):
            for core in range(cores):
                way = -step if mirrored and core else step
                pairs.append((at * cores + core, (at + way) % planes * cores + core))
        return lax.ppermute(array, ("z", "core"), pairs)

    def deliver(array):
        return lax.all_to_all(array, PLANE, split_axis=0, concat_axis=0, tiled=True)

    long1, short1 = hop(pool, 1, True), hop(pool, -1, True)

    where = (x, z, c, pools, planes, cores)
    place = jnp.stack([jnp.int32(value) for value in where])
    position = jnp.arange(max_blocks, dtype=jnp.int32)
    live = position[None, :] < prefix_blocks[:, None]
    owners = jnp.arange(owner_count, dtype=jnp.int32)
    table = jnp.sum(
        jnp.where(
            (block_owner[:, :, None] == owners[None, None, :]) & live[:, :, None],
            block_slot[:, :, None] + 1,
            0,
        ),
        axis=1,
    )

    both = jnp.concatenate([queries[0].reshape(tok_local, tensor_count, -1), stretch_kv[0]], axis=2)
    q_kv = lax.all_to_all(both, "tp", split_axis=1, concat_axis=0, tiled=True)
    tokens = tok_local * tensor_count
    q_kv = q_kv.reshape(tokens, -1)
    get = functools.partial(pick, place, table, peers=peers)
    step = functools.partial(
        attend, place, table, scale=scale, group=GROUP, head_dim=head_dim, tokens=tokens
    )
    long2, short2 = hop(long1, 1, True), hop(short1, -1, True)
    half_peers = peers // 2
    (start,) = get([pool], (((0, 4, 0), (0, 0, 0)),))
    start, q_kv = lax.optimization_barrier((start, q_kv))
    start = deliver(start)
    (send_near,) = get([long1, short1], (((0, 0, -1), (1, 0, 1)),))
    near = deliver(send_near)
    *state, query = step(q_kv, [start], ((0, (None, 0)),), None, False, after=[send_near])
    send_long, send_short, middle_sent = get(
        [long2, short2],
        (((0, 1, -2),), ((1, -1, 2),), ((0, 0, -2), (1, 0, 2))),
        after=[state[0]],
        cost=40,
    )
    far, _ = lax.optimization_barrier((start, near))
    long3, short3 = hop(send_long, 1, True), hop(send_short, -1, True)
    middle = deliver(middle_sent)
    far_up, far_down = hop(far[:half_peers, :1], 4, False), hop(far[half_peers:, :1], -4, False)
    third = join([long3, short3], cost=4)
    state = step(query, [near, middle], ((0, (-1, 1)), (0, (-2, 2))), state, False, after=[third], cost=60)
    third = deliver(third)
    (attended,) = step(
        query, [third, far_up, far_down], ((0, (-3, 3)), (0, (4,)), (half_peers, (4,))), state, True
    )
    attended = attended.reshape(tensor_count, tok_local, -1)
    return lax.all_to_all(attended, "tp", split_axis=0, concat_axis=2, tiled=True)


def solution(mesh):
    pools, seq, tensor = mesh.devices.shape
    fine = Mesh(mesh.devices.reshape(pools, seq // 2, 2, tensor), ("pool", "z", "core", "tp"))
    rows = ("pool", "z", "core")
    return jax.shard_map(
        local,
        mesh=fine,
        in_specs=(
            P(rows, "tp", None),
            P(rows, "tp", None, None),
            P(rows, None, "tp", None),
            P(),
            P(),
            P(),
        ),
        out_specs=P(rows, "tp", None),
        check_vma=False,
    )
```

```python
import functools
import math

import jax
import jax.numpy as jnp
from jax import lax
from jax.experimental import pallas as pl
from jax.experimental.pallas import tpu as pltpu
from jax.sharding import Mesh
from jax.sharding import PartitionSpec as P

QH = 64
KVH = 8
GROUP = QH // KVH
MASKED_SCORE = -1e30
PEERS = 8
PLANE = ("core", "pool")
ANY = pl.BlockSpec(memory_space=pltpu.HBM)
VMEM = pl.BlockSpec(memory_space=pltpu.VMEM)


def cost_of(microseconds):
    return pl.CostEstimate(
        flops=int(microseconds * 1.1e9), transcendentals=0, bytes_accessed=int(microseconds * 3.6e6)
    )


def pick_kernel(outputs, count, place, table, *refs):
    buffers, outs, sem = refs[:count], refs[-1 - len(outputs) : -1], refs[-1]
    x, z, c = place[0], place[1], place[2]
    planes, cores = place[4], place[5]
    way = 1 - 2 * c
    copies = []
    for out, columns in zip(outs, outputs):
        peers = out.shape[0]
        pools = peers // 2
        for column, (buffer, request_step, owner_step) in enumerate(columns):
            request_z = lax.rem(z + request_step * way + planes, planes)
            owner_z = lax.rem(z + owner_step * way + planes, planes)
            owner = (x * planes + owner_z) * cores + c
            for peer in range(peers):
                request = (peer % pools * planes + request_z) * cores + peer // pools
                slot = jnp.maximum(table[request, owner] - 1, 0)
                copy = pltpu.make_async_copy(buffers[buffer].at[slot], out.at[peer, column], sem)
                copy.start()
                copies.append(copy)
    for copy in copies:
        copy.wait()


def pick(place, table, buffers, outputs, peers, after=(), cost=4):
    block, dtype = buffers[0].shape[1:], buffers[0].dtype
    operands = list(buffers) + list(after)
    return pl.pallas_call(
        functools.partial(pick_kernel, outputs, len(buffers)),
        grid_spec=pltpu.PrefetchScalarGridSpec(
            num_scalar_prefetch=2,
            grid=(1,),
            in_specs=[ANY] * len(operands),
            out_specs=[pl.BlockSpec((peers, len(columns)) + block, lambda *_: (0, 0, 0, 0)) for columns in outputs],
            scratch_shapes=[pltpu.SemaphoreType.DMA],
        ),
        out_shape=[jax.ShapeDtypeStruct((peers, len(columns)) + block, dtype) for columns in outputs],
        cost_estimate=cost_of(cost),
    )(place, table, *operands)


def join_kernel(*refs):
    arrays, out, sem = refs[:-2], refs[-2], refs[-1]
    copies = [pltpu.make_async_copy(array, out.at[:, at : at + 1], sem) for at, array in enumerate(arrays)]
    for copy in copies:
        copy.start()
    for copy in copies:
        copy.wait()


def join(arrays, cost):
    peers, _, *block = arrays[0].shape
    shape = (peers, len(arrays), *block)
    return pl.pallas_call(
        join_kernel,
        grid=(1,),
        in_specs=[ANY] * len(arrays),
        out_specs=pl.BlockSpec(shape, lambda _: (0, 0, 0, 0)),
        scratch_shapes=[pltpu.SemaphoreType.DMA],
        out_shape=jax.ShapeDtypeStruct(shape, arrays[0].dtype),
        cost_estimate=cost_of(cost),
    )(*arrays)


def attend_kernel(rounds, chunk, first, last, scale, spare_operands, place, table, *refs):
    refs = list(refs)
    q_in = refs.pop(0)
    arrived = [refs.pop(0) for _ in rounds]
    if not first:
        acc_in, ml_in = refs.pop(0), refs.pop(0)
    del refs[:spare_operands]
    if last:
        out_ref = refs.pop(0)
    else:
        acc_out, ml_out = refs.pop(0), refs.pop(0)
    if first:
        turned_out = refs.pop(0)
    blocks, acc, ml, query_buffer, turned, sem, state_sem = refs
    x, z, c = place[0], place[1], place[2]
    pools, planes, cores = place[3], place[4], place[5]
    me = (x * planes + z) * cores + c
    group, head_dim, tokens = acc.shape
    block_len = arrived[0].shape[2]
    if first:
        width, pair = group * head_dim, 2 * head_dim
        tensor = place[6]
        own_from = q_in.shape[1] // (width + pair) * width
        heads = pl.ds(pl.multiple_of(tensor * width, width), width)
        own_at = pl.ds(pl.multiple_of(own_from + tensor * pair, pair), pair)
        loads = [
            pltpu.make_async_copy(q_in.at[:, heads], query_buffer.at[:, :width], state_sem),
            pltpu.make_async_copy(q_in.at[:, own_at], query_buffer.at[:, width:], state_sem),
        ]
    else:
        pairs = ((q_in, turned), (acc_in, acc), (ml_in, ml))
        loads = [pltpu.make_async_copy(source, target, state_sem) for source, target in pairs]
    for load in loads:
        load.start()

    def fetch(source, at):
        return pltpu.make_async_copy(source, blocks.at[pl.ds(at * block_len, block_len)], sem)

    count = jnp.int32(0)
    for array, (start, steps) in zip(arrived, rounds):
        for lane in range(array.shape[0]):
            core, sender = divmod(start + lane, PEERS // 2)
            way = 1 - 2 * core
            for column in range(array.shape[1]):
                if steps[column] is None:
                    continue
                owner_z = lax.rem(z + steps[column] * way + planes, planes)
                live = table[me, (sender * planes + owner_z) * cores + core] > 0

                @pl.when(live)
                def _():
                    fetch(array.at[lane, column], count).start()

                count = count + live.astype(jnp.int32)
    half = chunk // 2
    wholes = (count + half - 1) // chunk
    halves = (jnp.maximum(count - wholes * chunk, 0) + half - 1) // half
    held = wholes * chunk + halves * half
    spare = arrived[0].at[0, 0]

    def fill(at, carried):
        fetch(spare, at).start()
        return carried

    def drain(at, carried):
        fetch(spare, at).wait()
        return carried

    lax.fori_loop(count, held, fill, 0)

    def scores_of(head, keys):
        query = turned[head * head_dim : (head + 1) * head_dim, :]
        return jnp.dot(keys, query, preferred_element_type=jnp.float32)

    def absorb(pending):
        head, weights, values, shrink = pending
        add = jnp.dot(values, weights, preferred_element_type=jnp.float32)
        acc[head] = add if shrink is None else acc[head] * shrink + add

    def sweep(keys, values, mask, fresh):
        score, pending = scores_of(0, keys), None
        for head in range(group):
            ahead = scores_of(head + 1, keys) if head + 1 < group else None
            score = mask(score)
            top = jnp.max(score, axis=0, keepdims=True)
            shrink = None
            if not fresh:
                old = ml[0, head : head + 1, :]
                top = jnp.maximum(top, old)
                shrink = jnp.exp2((old - top) * scale)
            weights = jnp.exp2((score - top) * scale)
            total = jnp.sum(weights, axis=0, keepdims=True)
            ml[1, head : head + 1, :] = total if fresh else ml[1, head : head + 1, :] * shrink + total
            ml[0, head : head + 1, :] = top
            if pending is not None:
                absorb(pending)
            pending = (head, weights.astype(values.dtype), values, shrink)
            score = ahead
        absorb(pending)

    for load in loads:
        load.wait()
    if first:
        turned[...] = query_buffer[:, : group * head_dim].T
        own = query_buffer[:, group * head_dim :]
        key = lax.broadcasted_iota(jnp.int32, (tokens, tokens), 0)
        token = lax.broadcasted_iota(jnp.int32, (tokens, tokens), 1)
        sweep(own[:, :head_dim], own[:, head_dim:].T, lambda s: jnp.where(key <= token, s, MASKED_SCORE), True)
    lax.fori_loop(0, held, drain, 0)

    def take(base, length, sure):
        size = length * block_len
        kv = blocks[pl.ds(pl.multiple_of(base * block_len, half * block_len), size), :]

        def mask(score):
            parts = [score[: sure * block_len]]
            for b in range(sure, length):
                part = score[b * block_len : (b + 1) * block_len]
                parts.append(jnp.where(base + b < count, part, MASKED_SCORE))
            return jnp.concatenate(parts, axis=0)

        sweep(kv[:, :head_dim], kv[:, head_dim:].T, mask, False)

    def body(at, carried):
        take(at * chunk, chunk, half + 1)
        return carried

    lax.fori_loop(0, wholes, body, 0)

    @pl.when(halves > 0)
    def _():
        take(wholes * chunk, half, 1)

    if last:
        for head in range(group):
            done = acc[head] / ml[1, head : head + 1, :]
            out_ref[:, head * head_dim : (head + 1) * head_dim] = done.T.astype(out_ref.dtype)
    else:
        pairs = [(acc, acc_out), (ml, ml_out)] + ([(turned, turned_out)] if first else [])
        stores = [pltpu.make_async_copy(source, target, state_sem) for source, target in pairs]
        for store in stores:
            store.start()
        for store in stores:
            store.wait()


def attend(place, table, query, arrived, rounds, state, last, scale, group, head_dim, tokens, after=(), cost=8, chunk=8):
    first = state is None
    dtype = arrived[0].dtype
    slots = sum(array.shape[0] * array.shape[1] for array in arrived)
    slots = (slots + chunk - 1) // chunk * chunk
    block_len = arrived[0].shape[2]
    operands = [query] + list(arrived) + ([] if first else list(state)) + list(after)
    kept = range(1) if first else (0, 1 + len(arrived), 2 + len(arrived))
    for at in kept:
        operands[at] = pltpu.with_memory_space_constraint(operands[at], pltpu.HBM)
    acc = ((group, head_dim, tokens), jnp.float32)
    ml = ((2, group, tokens), jnp.float32)
    turned = ((group * head_dim, tokens), dtype)
    outs = [((tokens, group * head_dim), dtype)] if last else [acc, ml]
    if first:
        outs.append(turned)
    return pl.pallas_call(
        functools.partial(
            attend_kernel, rounds, chunk, first, last, scale * math.log2(math.e), len(after)
        ),
        grid_spec=pltpu.PrefetchScalarGridSpec(
            num_scalar_prefetch=2,
            grid=(1,),
            in_specs=[ANY] * len(operands),
            out_specs=[VMEM if last else ANY] * len(outs),
            scratch_shapes=[
                pltpu.VMEM((slots * block_len, 2 * head_dim), dtype),
                pltpu.VMEM(*acc),
                pltpu.VMEM(*ml),
                pltpu.VMEM((tokens, (group + 2) * head_dim) if first else (16, 128), dtype),
                pltpu.VMEM(*turned),
                pltpu.SemaphoreType.DMA,
                pltpu.SemaphoreType.DMA,
            ],
        ),
        out_shape=[(jax.ShapeDtypeStruct if last else pltpu.HBM)(*out) for out in outs],
        compiler_params=pltpu.CompilerParams(vmem_limit_bytes=20 * 1024 * 1024),
        cost_estimate=cost_of(cost),
    )(place, table, *operands)


def local(queries, stretch_kv, pool_kv, prefix_blocks, block_owner, block_slot):
    pools, planes, cores = lax.axis_size("pool"), lax.axis_size("z"), lax.axis_size("core")
    x, z, c = lax.axis_index("pool"), lax.axis_index("z"), lax.axis_index("core")
    tensor_count = lax.axis_size("tp")
    owner_count = pools * planes * cores
    peers = pools * cores
    tok_local = queries.shape[1]
    block_len, pair = pool_kv.shape[1], pool_kv.shape[3]
    head_dim = pair // 2
    scale = 1.0 / math.sqrt(head_dim)
    max_blocks = block_owner.shape[1]
    pool = pool_kv.reshape(-1, block_len, pair)

    def hop(array, step, mirrored):
        pairs = []
        for at in range(planes):
            for core in range(cores):
                way = -step if mirrored and core else step
                pairs.append((at * cores + core, (at + way) % planes * cores + core))
        return lax.ppermute(array, ("z", "core"), pairs)

    def deliver(array):
        return lax.all_to_all(array, PLANE, split_axis=0, concat_axis=0, tiled=True)

    long1, short1 = hop(pool, 1, True), hop(pool, -1, True)

    where = (x, z, c, pools, planes, cores, lax.axis_index("tp"))
    place = jnp.stack([jnp.int32(value) for value in where])
    position = jnp.arange(max_blocks, dtype=jnp.int32)
    live = position[None, :] < prefix_blocks[:, None]
    owners = jnp.arange(owner_count, dtype=jnp.int32)
    table = jnp.sum(
        jnp.where(
            (block_owner[:, :, None] == owners[None, None, :]) & live[:, :, None],
            block_slot[:, :, None] + 1,
            0,
        ),
        axis=1,
    )

    both = jnp.concatenate([queries[0], stretch_kv[0].reshape(tok_local, -1)], axis=1)
    q_kv = lax.all_gather(both, "tp", axis=0, tiled=True)
    tokens = q_kv.shape[0]
    get = functools.partial(pick, place, table, peers=peers)
    step = functools.partial(
        attend, place, table, scale=scale, group=GROUP, head_dim=head_dim, tokens=tokens
    )
    long2, short2 = hop(long1, 1, True), hop(short1, -1, True)
    half_peers = peers // 2
    (start,) = get([pool], (((0, 4, 0), (0, 0, 0)),))
    start = deliver(start)
    (send_near,) = get([long1, short1], (((0, 0, -1), (1, 0, 1)),), after=[start], cost=60)
    near = deliver(send_near)
    send_long, send_short, middle_sent = get(
        [long2, short2],
        (((0, 1, -2),), ((1, -1, 2),), ((0, 0, -2), (1, 0, 2))),
        cost=40,
    )
    far, _ = lax.optimization_barrier((start, near))
    long3, short3 = hop(send_long, 1, True), hop(send_short, -1, True)
    middle = deliver(middle_sent)
    far_up, far_down = hop(far[:half_peers, :1], 4, False), hop(far[half_peers:, :1], -4, False)
    third = join([long3, short3], cost=4)
    *state, query = step(
        q_kv, [start, near, middle], ((0, (None, 0)), (0, (-1, 1)), (0, (-2, 2))), None, False, after=[third], cost=60
    )
    third = deliver(third)
    (attended,) = step(
        query, [third, far_up, far_down], ((0, (-3, 3)), (0, (4,)), (half_peers, (4,))), state, True
    )
    attended = attended.reshape(tensor_count, tok_local, -1)
    return lax.all_to_all(attended, "tp", split_axis=0, concat_axis=2, tiled=True)


def solution(mesh):
    pools, seq, tensor = mesh.devices.shape
    fine = Mesh(mesh.devices.reshape(pools, seq // 2, 2, tensor), ("pool", "z", "core", "tp"))
    rows = ("pool", "z", "core")
    return jax.shard_map(
        local,
        mesh=fine,
        in_specs=(
            P(rows, "tp", None),
            P(rows, "tp", None, None),
            P(rows, None, "tp", None),
            P(),
            P(),
            P(),
        ),
        out_specs=P(rows, "tp", None),
        check_vma=False,
    )
```
